32 devices in a mesh: dp: 8 (over y, x, core), mp: 4 (over z).
Axes of the slice: x: 2, y: 2, z: 4, core: 2. Of those that a mesh axis runs over, the one named last changes fastest.
Arguments:
- inputs: bfloat16 [8192, 768], P(('dp', 'mp')), may hold values from -6 to 6
- cotangent: bfloat16 [8192, 768], P(('dp', 'mp')), may hold values from -6 to 6
- doc_lengths: int32 [8, 4], P('dp'), may hold values from 1 to 832, as said below
- first_gain: float32 [768], replicated, may hold values from 0.1 to 1.9
- first_shift: float32 [768], replicated, may hold values from -1.5 to 1.5
- qkv_weight: bfloat16 [768, 3, 768], P('dp', None, 'mp'), may hold values from -0.21875 to 0.21875
- qv_bias: float32 [2, 768], P(None, 'mp'), may hold values from -1.5 to 1.5
- out_weight: bfloat16 [768, 768], P('mp', 'dp'), may hold values from -1.75 to 1.75
- out_bias: float32 [768], replicated, may hold values from -1.5 to 1.5
- second_gain: float32 [768], replicated, may hold values from 0.1 to 1.9
- second_shift: float32 [768], replicated, may hold values from -1.5 to 1.5
- up_weight: bfloat16 [768, 3072], P('dp', 'mp'), may hold values from -0.21875 to 0.21875
- up_bias: float32 [3072], P('mp'), may hold values from -1.5 to 1.5
- down_weight: bfloat16 [3072, 768], P('mp', 'dp'), may hold values from -0.109375 to 0.109375
- down_bias: float32 [768], replicated, may hold values from -1.5 to 1.5
Outputs:
- outputs: bfloat16 [8192, 768], P(('dp', 'mp'))
- grad_inputs: bfloat16 [8192, 768], P(('dp', 'mp'))
- grad_first_gain: float32 [768], replicated
- grad_first_shift: float32 [768], replicated
- grad_qkv_weight: float32 [768, 3, 768], P('dp', None, 'mp')
- grad_qv_bias: float32 [2, 768], P(None, 'mp')
- grad_out_weight: float32 [768, 768], P('mp', 'dp')
- grad_out_bias: float32 [768], replicated
- grad_second_gain: float32 [768], replicated
- grad_second_shift: float32 [768], replicated
- grad_up_weight: float32 [768, 3072], P('dp', 'mp')
- grad_up_bias: float32 [3072], P('mp')
- grad_down_weight: float32 [3072, 768], P('mp', 'dp')
- grad_down_bias: float32 [768], replicated
The draws below stay inside these ranges and needn't reach their ends.
Inputs may be any that keep to these rules, and one draw needn't show every extreme that they name: `doc_lengths`: in each block one document, at a place drawn from the seed, has exactly 832 tokens and the others 1 to 64; the lengths of a block sum to at most 1024, and the rest of the block is padding.
All inputs are finite; a program needn't handle non-finite values.
Results may differ from the reference program's by a relative error of at most 0.012.
The reference program's roundings to bfloat16 on the way count: a program that leaves them out, or rounds other values in their place, can miss the bound.
Values may be sent and summed in bfloat16 or wider, within the bound.
A program may use at most 128 MiB of HBM per device.

```python
import jax
import jax.numpy as jnp
from jax import lax

D = 768
HEADS = 12
HEAD_DIM = 64
FF = 3072
DOCS = 4
SEQ = 1024
BLOCKS = 8
ROWS = 8192


def draw_doc_lengths(key, part):
    key = jax.random.fold_in(key, 11)
    short_key, place_key = jax.random.split(key)
    shorter = jax.random.randint(short_key, (BLOCKS, DOCS), 1, SEQ // 16 + 1)
    chosen = jax.random.randint(place_key, (BLOCKS, 1), 0, DOCS)
    columns = jnp.arange(DOCS, dtype=jnp.int32)[None, :]
    longest = 13 * SEQ // 16
    return jnp.where(columns == chosen, longest, shorter).astype(jnp.int32)


def with_spikes(entries, rng, source, target, parts, factor):
    def block_of(axis_at):
        return (jnp.arange(entries.shape[axis_at]) // (entries.shape[axis_at] // parts)).reshape((-1,) + (1,) * (entries.ndim - 1 - axis_at))

    one_side = jax.random.permutation(rng, parts)[block_of(target)]
    far = (block_of(target) + parts // 2) % parts
    return jnp.where((block_of(source) == one_side) | (block_of(source) == far), factor * entries, entries)


def block_scale(key, shape, pieces, least, top_value):
    factor_of, own = 1.0, jax.random.fold_in(key, 6)
    for position, parts in pieces:
        steps = jnp.exp(jax.random.uniform(jax.random.fold_in(own, position), (parts,), jnp.float32, least / len(pieces), top_value / len(pieces)))
        factor_of = factor_of * jnp.repeat(steps, shape[position] // parts).reshape([-1 if axis == position else 1 for axis in range(len(shape))])
    return factor_of


def scatter_about(rng, shape, scale, limit, shards=(), held_as=jnp.bfloat16):
    drawn = scale * jax.random.normal(rng, shape, jnp.float32)
    if shards:
        drawn = drawn * block_scale(rng, shape, shards, -0.22, 0.18)
    return jnp.clip(drawn, -limit, limit).astype(held_as)


def bell_draw_with(own_key, shape, deviation, limit, shards, heavy, kind=jnp.bfloat16):
    values = deviation * jax.random.normal(own_key, shape, jnp.float32)
    if shards:
        values = values * block_scale(own_key, shape, shards, -0.22, 0.18)
    return jnp.clip(with_spikes(values, jax.random.fold_in(own_key, 3), *heavy), -limit, limit).astype(kind)


def setup_inputs(seed: int = 0) -> dict:
    key_of = jax.random.split(jax.random.key(seed), 16)
    inputs = scatter_about(key_of[0], (ROWS, D), 1.0, 6.0, ((0, 32),))
    cotangent = bell_draw_with(key_of[1], (ROWS, D), 1.0, 6.0, ((0, 32),), (0, 1, 32, 2.75))
    doc_lengths = draw_doc_lengths(jax.random.fold_in(key_of[15], 71), 0)
    first_gain = jnp.clip(1.0 + 0.18 * jax.random.normal(key_of[3], (D,), jnp.float32), 0.1, 1.9)
    first_shift = scatter_about(key_of[4], (D,), 0.3, 1.5, (), jnp.float32)
    qkv_weight = scatter_about(key_of[5], (D, 3, D), D ** -0.5, 0.21875, ((0, 8), (2, 4)))
    qv_bias = scatter_about(key_of[6], (2, D), 0.3, 1.5, ((1, 4),), jnp.float32)
    out_weight = scatter_about(key_of[7], (D, D), (max(D // 64, 1)) ** -0.5, 1.75, ((0, 4), (1, 8)))
    out_bias = scatter_about(key_of[8], (D,), 0.3, 1.5, (), jnp.float32)
    second_gain = jnp.clip(1.0 + 0.18 * jax.random.normal(key_of[9], (D,), jnp.float32), 0.1, 1.9)
    second_shift = scatter_about(key_of[10], (D,), 0.3, 1.5, (), jnp.float32)
    up_weight = scatter_about(key_of[11], (D, FF), D ** -0.5, 0.21875, ((0, 8), (1, 4)))
    up_bias = scatter_about(key_of[12], (FF,), 0.3, 1.5, ((0, 4),), jnp.float32)
    down_weight = scatter_about(key_of[13], (FF, D), FF ** -0.5, 0.109375, ((0, 4), (1, 8)))
    down_bias = scatter_about(key_of[14], (D,), 0.3, 1.5, (), jnp.float32)
    return dict(inputs=inputs, cotangent=cotangent, doc_lengths=doc_lengths, first_gain=first_gain, first_shift=first_shift, qkv_weight=qkv_weight, qv_bias=qv_bias, out_weight=out_weight, out_bias=out_bias, second_gain=second_gain, second_shift=second_shift, up_weight=up_weight, up_bias=up_bias, down_weight=down_weight, down_bias=down_bias)


@jax.custom_vjp
def low(v):
    return lax.optimization_barrier(v.astype(jnp.bfloat16)).astype(jnp.float32)

@jax.custom_vjp
def low_back(v):
    return v

def low_keep(v):
    return (low(v), None)

def low_pass(kept, grad):
    return (grad,)

def back_keep(v):
    return (v, None)

def back_low(kept, grad):
    return (low(grad),)
low.defvjp(low_keep, low_pass)
low_back.defvjp(back_keep, back_low)
EPSILON = 1e-05
HIGHEST = lax.Precision.HIGHEST

def layer_norm(values, gain, shift):
    center = values - lax.optimization_barrier(jnp.mean(values, axis=-1, keepdims=True))
    spread = lax.optimization_barrier(jnp.mean(center * center, axis=-1, keepdims=True))
    return center * lax.rsqrt(spread + EPSILON) * gain + shift

def layout(lengths):
    ends = jnp.cumsum(lengths).astype(jnp.int32)
    places = jnp.arange(SEQ, dtype=jnp.int32)
    segment = lax.optimization_barrier(jnp.sum((places[:, None] >= ends[None, :]).astype(jnp.int32), axis=1))
    valid = (places < ends[-1]).astype(jnp.float32)
    return (segment, valid)

def attention(queries, keys, values, segment):
    width = min(512, SEQ)
    count = SEQ // width
    places = jnp.arange(SEQ, dtype=jnp.int32)

    def block(item):
        query_block, first = item
        rows_here = first + jnp.arange(width, dtype=jnp.int32)
        rows_segment = lax.dynamic_slice_in_dim(segment, first, width)
        allowed = (rows_segment[:, None] == segment[None, :]) & (rows_here[:, None] >= places[None, :])
        scores = low_back(jnp.einsum('qhe,khe->hqk', query_block, keys, precision=HIGHEST))
        scores = jnp.where(allowed[None], scores, -1e+30)
        weights = low(jax.nn.softmax(scores, axis=-1))
        return jnp.einsum('hqk,khe->qhe', weights, values, precision=HIGHEST)
    starts = jnp.arange(count, dtype=jnp.int32) * width
    blocks_out = lax.map(jax.checkpoint(block), (queries.reshape(count, width, HEADS, HEAD_DIM), starts))
    return blocks_out.reshape(SEQ, HEADS, HEAD_DIM)

def block_forward(inputs, weights, segment):
    first_gain, first_shift, qkv_weight, qv_bias, out_weight, out_bias, second_gain, second_shift, up_weight, up_bias, down_weight, down_bias = weights
    factor = HEAD_DIM ** (-0.5)
    normed_one = low(layer_norm(inputs, first_gain, first_shift))
    mixed = jnp.einsum('td,dcf->tcf', normed_one, qkv_weight, precision=HIGHEST)
    queries = low(low_back((mixed[:, 0] + qv_bias[0]) * factor)).reshape(SEQ, HEADS, HEAD_DIM)
    keys = low(low_back(mixed[:, 1])).reshape(SEQ, HEADS, HEAD_DIM)
    values = low(low_back(mixed[:, 2] + qv_bias[1])).reshape(SEQ, HEADS, HEAD_DIM)
    context = low(low_back(attention(queries, keys, values, segment))).reshape(SEQ, D)
    hidden = inputs + low_back(jnp.dot(context, out_weight, precision=HIGHEST)) + out_bias
    normed_two = low(layer_norm(hidden, second_gain, second_shift))
    upper = low_back(jnp.dot(normed_two, up_weight, precision=HIGHEST) + up_bias)
    active = low(jax.nn.gelu(upper, approximate=True))
    return hidden + low_back(jnp.dot(active, down_weight, precision=HIGHEST)) + down_bias

def reference(inputs, cotangent, doc_lengths, first_gain, first_shift, qkv_weight, qv_bias, out_weight, out_bias, second_gain, second_shift, up_weight, up_bias, down_weight, down_bias):
    params = tuple((item.astype(jnp.float32) for item in (first_gain, first_shift, qkv_weight, qv_bias, out_weight, out_bias, second_gain, second_shift, up_weight, up_bias, down_weight, down_bias)))
    blocks_in = inputs.astype(jnp.float32).reshape(BLOCKS, SEQ, D)
    blocks_cot = cotangent.astype(jnp.float32).reshape(BLOCKS, SEQ, D)

    def one_block(totals, item):
        block_in, block_cot, lengths = item
        segment, valid = layout(lengths)

        def forward(values, *weights):
            return block_forward(values, weights, segment)
        result, pull = jax.vjp(forward, block_in, *params)
        grads = pull(block_cot * valid[:, None])
        totals = tuple((left + right for left, right in zip(totals, grads[1:])))
        return (totals, (result, grads[0]))
    zeros = tuple((jnp.zeros_like(item) for item in params))
    totals, (results, grad_blocks) = lax.scan(one_block, zeros, (blocks_in, blocks_cot, doc_lengths))
    g_first_gain, g_first_shift, g_qkv_weight, g_qv_bias, g_out_weight, g_out_bias, g_second_gain, g_second_shift, g_up_weight, g_up_bias, g_down_weight, g_down_bias = totals
    return (results.reshape(ROWS, D).astype(jnp.bfloat16), grad_blocks.reshape(ROWS, D).astype(jnp.bfloat16), g_first_gain, g_first_shift, g_qkv_weight, g_qv_bias, g_out_weight, g_out_bias, g_second_gain, g_second_shift, g_up_weight, g_up_bias, g_down_weight, g_down_bias)
```

```python
import jax
import jax.numpy as jnp
from jax import lax
from jax.sharding import PartitionSpec as P

HEAD_DIM = 64


EPSILON = 1e-05


def layer_norm(values, gain, shift):
    center = values - jnp.mean(values, axis=-1, keepdims=True)
    spread = jnp.mean(center * center, axis=-1, keepdims=True)
    return center * lax.rsqrt(spread + EPSILON) * gain + shift


def smooth_gate(values):
    return jax.nn.gelu(values, approximate=True)


def swap(values, axis, mask):
    count = lax.axis_size(axis)
    return lax.ppermute(values, axis, [(i, i ^ mask) for i in range(count)])


def bits_of(axis):
    return [1 << k for k in range(lax.axis_size(axis).bit_length() - 1)]


def orders(axis):
    bits = bits_of(axis)
    return bits[1:] + bits[:1], bits[:0:-1] + bits[:1]


def gather_blocks(block, axis, order):
    me = lax.axis_index(axis)
    held = block[None]
    for bit in order:
        held = jnp.concatenate([held, swap(held, axis, bit)], axis=0)
    parts = []
    for j in range(lax.axis_size(axis)):
        relative = me ^ j
        slot = sum(((relative // bit) % 2) * (1 << k) for k, bit in enumerate(order))
        parts.append(lax.dynamic_index_in_dim(held, slot, 0, keepdims=False))
    return jnp.concatenate(parts, axis=0)


def scatter_blocks(total, axis, order):
    me = lax.axis_index(axis)
    left = bits_of(axis)[::-1]
    rows = total.shape[0] // lax.axis_size(axis)
    total = total.reshape((2,) * len(left) + (rows,) + total.shape[1:])
    for bit in order[::-1]:
        place = left.index(bit)
        side = (me // bit) % 2
        sent = lax.dynamic_index_in_dim(total, 1 - side, place, keepdims=False)
        kept = lax.dynamic_index_in_dim(total, side, place, keepdims=False)
        total = kept + swap(sent.astype(jnp.bfloat16), axis, bit).astype(jnp.float32)
        left.remove(bit)
    return total


def gather_chunks(chunk):
    return [chunk] + [swap(chunk, "mp", r) for r in range(1, lax.axis_size("mp"))]


def scatter_chunks(product):
    count = lax.axis_size("mp")
    arrived = [swap(product(r).astype(jnp.bfloat16), "mp", r) for r in range(count - 1, 0, -1)]
    total = product(0)
    for piece in arrived:
        total = total + piece.astype(jnp.float32)
    return total


def sum_over(values, axis):
    for bit in bits_of(axis):
        values = values + swap(values, axis, bit)
    return values


def after(values, *earlier):
    return lax.optimization_barrier((values, *earlier))[0]


def join(chunks):
    return jnp.concatenate(chunks, axis=0)


def attend_forward(queries, keys, values, segment, places, width):
    length, heads_here, head_size = queries.shape
    contexts, logsums = [], []
    for first in range(0, length, width):
        part = slice(first, first + width)
        allowed = (segment[part, None] == segment[None, :]) & (places[part, None] >= places[None, :])
        scores = jnp.einsum(
            "qhe,khe->hqk", queries[part], keys, preferred_element_type=jnp.float32
        )
        scores = jnp.where(allowed[None], scores, -1e30)
        largest = jnp.max(scores, axis=-1, keepdims=True)
        exponent = jnp.exp(scores - largest)
        total = jnp.sum(exponent, axis=-1, keepdims=True)
        weights = (exponent / total).astype(jnp.bfloat16)
        context = jnp.einsum("hqk,khe->qhe", weights, values, preferred_element_type=jnp.float32)
        contexts.append(context.astype(jnp.bfloat16).reshape(width, heads_here * head_size))
        logsums.append(largest + jnp.log(total))
    return join(contexts), logsums


def attend_backward(queries, keys, values, grad_context, logsums, segment, places, width):
    length, heads_here, head_size = queries.shape
    grad_keys = jnp.zeros(keys.shape, jnp.float32)
    grad_values = jnp.zeros(keys.shape, jnp.float32)
    grad_queries = []
    for index, first in enumerate(range(0, length, width)):
        part = slice(first, first + width)
        allowed = (segment[part, None] == segment[None, :]) & (places[part, None] >= places[None, :])
        query_block, grad_block = queries[part], grad_context[part]
        scores = jnp.einsum("qhe,khe->hqk", query_block, keys, preferred_element_type=jnp.float32)
        scores = jnp.where(allowed[None], scores, -1e30)
        softmax_weights = jnp.exp(scores - logsums[index])
        grad_values = grad_values + jnp.einsum(
            "hqk,qhe->khe",
            softmax_weights.astype(jnp.bfloat16),
            grad_block,
            preferred_element_type=jnp.float32,
        )
        grad_weights = jnp.einsum(
            "qhe,khe->hqk", grad_block, values, preferred_element_type=jnp.float32
        )
        inner = jnp.sum(softmax_weights * grad_weights, axis=-1, keepdims=True)
        grad_scores = (softmax_weights * (grad_weights - inner)).astype(jnp.bfloat16)
        grad_query = jnp.einsum(
            "hqk,khe->qhe", grad_scores, keys, preferred_element_type=jnp.float32
        )
        grad_keys = grad_keys + jnp.einsum(
            "hqk,qhe->khe", grad_scores, query_block, preferred_element_type=jnp.float32
        )
        grad_queries.append(grad_query.astype(jnp.bfloat16).reshape(width, heads_here * head_size))
    return (
        join(grad_queries),
        grad_keys.astype(jnp.bfloat16).reshape(length, heads_here * head_size),
        grad_values.astype(jnp.bfloat16).reshape(length, heads_here * head_size),
    )


ROWS_DIM = (((0,), (0,)), ((), ()))
COLS_DIM = (((1,), (1,)), ((), ()))
f32 = jnp.float32


def dot(left, right):
    return jnp.dot(left, right, preferred_element_type=f32)


def dot_cols(left, right):
    return lax.dot_general(left, right, COLS_DIM, preferred_element_type=f32)


def dot_rows(left, right):
    return lax.dot_general(left, right, ROWS_DIM, preferred_element_type=f32)


def local(
    inputs,
    cotangent,
    doc_lengths,
    first_gain,
    first_shift,
    qkv_weight,
    qv_bias,
    out_weight,
    out_bias,
    second_gain,
    second_shift,
    up_weight,
    up_bias,
    down_weight,
    down_bias,
):
    rows_here = inputs.shape[0]
    group = lax.axis_size("mp")
    length = rows_here * group
    width = min(512, length)
    cols_here = qkv_weight.shape[2]
    heads_here = cols_here // HEAD_DIM
    factor = HEAD_DIM ** (-0.5)
    me = lax.axis_index("mp")
    order_a, order_b = orders("dp")
    ends = jnp.cumsum(doc_lengths[0])
    steps = jnp.arange(rows_here, dtype=jnp.int32)
    places = join([(me ^ r) * rows_here + steps for r in range(group)])
    segment = jnp.sum((places[:, None] >= ends[None, :]).astype(jnp.int32), axis=1)
    valid = (places[:rows_here] < ends[-1]).astype(f32)

    start_values = inputs.astype(f32)
    normed_one = layer_norm(start_values, first_gain, first_shift).astype(jnp.bfloat16)
    chunks_one = gather_chunks(normed_one)
    whole_qkv = gather_blocks(
        qkv_weight.reshape(qkv_weight.shape[0], 3 * cols_here), "dp", order_a
    )
    late_out, late_up, late_down = out_weight.T, up_weight, down_weight.T
    late_out, late_up, late_down, whole_qkv = lax.optimization_barrier(
        (late_out, late_up, late_down, whole_qkv)
    )
    whole_out = gather_blocks(late_out, "dp", order_b)
    whole_up = gather_blocks(late_up, "dp", order_a)
    whole_down = gather_blocks(late_down, "dp", order_b)

    mixed = [dot(chunk, whole_qkv) for chunk in chunks_one]
    queries = join(
        [((m[:, :cols_here] + qv_bias[0]) * factor).astype(jnp.bfloat16) for m in mixed]
    ).reshape(length, heads_here, HEAD_DIM)
    keys_all = join([m[:, cols_here : 2 * cols_here].astype(jnp.bfloat16) for m in mixed]).reshape(
        length, heads_here, HEAD_DIM
    )
    values_all = join(
        [(m[:, 2 * cols_here :] + qv_bias[1]).astype(jnp.bfloat16) for m in mixed]
    ).reshape(length, heads_here, HEAD_DIM)
    context, logsum = attend_forward(queries, keys_all, values_all, segment, places, width)

    grad_out = cotangent.astype(f32) * valid[:, None]
    grad_out_low = after(grad_out.astype(jnp.bfloat16), queries, keys_all, values_all)
    chunks_grad = gather_chunks(grad_out_low)

    def rows_of(values, r):
        return values[r * rows_here : (r + 1) * rows_here]

    hidden = (
        start_values
        + scatter_chunks(lambda r: dot_cols(rows_of(context, r), whole_out))
        + out_bias
    )
    normed_two = layer_norm(hidden, second_gain, second_shift).astype(jnp.bfloat16)
    chunks_two = gather_chunks(normed_two)
    active, grad_upper = [], []
    for r in range(group):
        upper = dot(chunks_two[r], whole_up) + up_bias
        gate_value, gate_pull = jax.vjp(smooth_gate, upper)
        active.append(gate_value.astype(jnp.bfloat16))
        grad_active = dot(chunks_grad[r], whole_down)
        grad_upper.append(gate_pull(grad_active)[0].astype(jnp.bfloat16))
    grad_normed_two = scatter_chunks(lambda r: dot_cols(grad_upper[r], whole_up))

    norm_value, second_pull = jax.vjp(layer_norm, hidden, second_gain, second_shift)
    grad_hidden_norm, grad_second_gain, grad_second_shift = second_pull(grad_normed_two)
    grad_hidden = grad_out + grad_hidden_norm
    chunks_hidden = gather_chunks(grad_hidden.astype(jnp.bfloat16))
    grad_context = join([dot(chunk, whole_out).astype(jnp.bfloat16) for chunk in chunks_hidden])

    all_active, all_grad_upper = join(active), join(grad_upper)
    grad_down_weight = dot_rows(join(chunks_grad), all_active)
    grad_up_weight = dot_rows(join(chunks_two), all_grad_upper)
    grad_up_bias = jnp.sum(all_grad_upper, axis=0, dtype=f32)
    grad_out_weight = dot_rows(join(chunks_hidden), context)
    shard_down = scatter_blocks(grad_down_weight, "dp", order_b).T
    shard_up = scatter_blocks(grad_up_weight, "dp", order_a)
    shard_out = scatter_blocks(grad_out_weight, "dp", order_b).T

    early = jnp.concatenate(
        [
            grad_second_gain,
            grad_second_shift,
            jnp.sum(grad_hidden, axis=0),
            jnp.sum(grad_out, axis=0),
        ]
    )
    model = first_gain.shape[0]
    early = sum_over(jnp.concatenate([sum_over(early, "mp"), grad_up_bias]), "dp")

    late_active = list(lax.optimization_barrier((*active, grad_context)))
    grad_context = late_active.pop()
    result = (
        hidden + scatter_chunks(lambda r: dot_cols(late_active[r], whole_down)) + down_bias
    ).astype(jnp.bfloat16)

    grad_queries, grad_keys, grad_values = attend_backward(
        queries,
        keys_all,
        values_all,
        grad_context.reshape(length, heads_here, HEAD_DIM),
        logsum,
        segment,
        places,
        width,
    )
    grad_queries = grad_queries * factor
    grad_mixed = jnp.concatenate([grad_queries, grad_keys, grad_values], axis=1)
    grad_normed_one = scatter_chunks(lambda r: dot_cols(rows_of(grad_mixed, r), whole_qkv))
    grad_qkv_weight = dot_rows(join(chunks_one), grad_mixed)
    shard_qkv = scatter_blocks(grad_qkv_weight, "dp", order_a).reshape(qkv_weight.shape)
    grad_qv_bias = jnp.concatenate(
        [jnp.sum(grad_queries, axis=0, dtype=f32), jnp.sum(grad_values, axis=0, dtype=f32)]
    )
    first_value, first_pull = jax.vjp(layer_norm, start_values, first_gain, first_shift)
    grad_start_norm, grad_first_gain, grad_first_shift = first_pull(grad_normed_one)
    grad_inputs = (grad_hidden + grad_start_norm).astype(jnp.bfloat16)
    late = sum_over(jnp.concatenate([grad_first_gain, grad_first_shift]), "mp")
    late = sum_over(jnp.concatenate([late, grad_qv_bias]), "dp")
    return (
        result,
        grad_inputs,
        late[:model],
        late[model : 2 * model],
        shard_qkv,
        late[2 * model :].reshape(2, cols_here),
        shard_out,
        early[2 * model : 3 * model],
        early[:model],
        early[model : 2 * model],
        shard_up,
        early[4 * model :],
        shard_down,
        early[3 * model : 4 * model],
    )


def solution(mesh):
    placed = (
        P(("dp", "mp"), None),
        P(("dp", "mp"), None),
        P("dp", None),
        P(),
        P(),
        P("dp", None, "mp"),
        P(None, "mp"),
        P("mp", "dp"),
        P(),
        P(),
        P(),
        P("dp", "mp"),
        P("mp"),
        P("mp", "dp"),
        P(),
    )
    return jax.shard_map(
        local,
        mesh=mesh,
        in_specs=placed,
        out_specs=(
            P(("dp", "mp"), None),
            P(("dp", "mp"), None),
            P(),
            P(),
            P("dp", None, "mp"),
            P(None, "mp"),
            P("mp", "dp"),
            P(),
            P(),
            P(),
            P("dp", "mp"),
            P("mp"),
            P("mp", "dp"),
            P(),
        ),
        check_vma=False,
    )
```

```python
import jax
import jax.numpy as jnp
from jax import lax
from jax.sharding import PartitionSpec as P

HEAD_DIM = 64


EPSILON = 1e-05


def layer_norm(values, gain, shift):
    center = values - jnp.mean(values, axis=-1, keepdims=True)
    spread = jnp.mean(center * center, axis=-1, keepdims=True)
    return center * lax.rsqrt(spread + EPSILON) * gain + shift


def smooth_gate(values):
    return jax.nn.gelu(values, approximate=True)


def swap(values, axis, mask):
    count = lax.axis_size(axis)
    return lax.ppermute(values, axis, [(i, i ^ mask) for i in range(count)])


def bits_of(axis):
    return [1 << k for k in range(lax.axis_size(axis).bit_length() - 1)]


def orders(axis):
    bits = bits_of(axis)
    return bits[1:] + bits[:1], bits[:0:-1] + bits[:1]


def gather_blocks(block, axis, order):
    me = lax.axis_index(axis)
    held = block[None]
    for bit in order:
        held = jnp.concatenate([held, swap(held, axis, bit)], axis=0)
    parts = []
    for j in range(lax.axis_size(axis)):
        relative = me ^ j
        slot = sum(((relative // bit) % 2) * (1 << k) for k, bit in enumerate(order))
        parts.append(lax.dynamic_index_in_dim(held, slot, 0, keepdims=False))
    return jnp.concatenate(parts, axis=0)


def scatter_product(left, right, axis, order):
    me = lax.axis_index(axis)
    bits = bits_of(axis)[::-1]
    rows = left.shape[1] // lax.axis_size(axis)
    split = left.reshape(left.shape[:1] + (2,) * len(bits) + (rows,))
    total = None
    for bit in order[::-1]:
        place = bits.index(bit)
        side = (me // bit) % 2
        if total is None:
            sent, kept = (
                dot_rows(
                    lax.dynamic_index_in_dim(split, half, 1 + place, keepdims=False).reshape(
                        left.shape[0], left.shape[1] // 2
                    ),
                    right,
                )
                for half in (1 - side, side)
            )
        else:
            sent = lax.dynamic_index_in_dim(total, 1 - side, place, keepdims=False)
            kept = lax.dynamic_index_in_dim(total, side, place, keepdims=False)
        total = kept + swap(sent.astype(jnp.bfloat16), axis, bit).astype(f32)
        bits.remove(bit)
        total = total.reshape((2,) * len(bits) + (rows,) + right.shape[1:])
    return total


def gather_chunks(chunk):
    return [chunk] + [swap(chunk, "mp", r) for r in range(1, lax.axis_size("mp"))]


def scatter_chunks(product):
    count = lax.axis_size("mp")
    arrived = [swap(product(r).astype(jnp.bfloat16), "mp", r) for r in range(count - 1, 0, -1)]
    total = product(0)
    for piece in arrived:
        total = total + piece.astype(jnp.float32)
    return total


def sum_over(values, axis):
    bits = bits_of(axis)
    while bits:
        first, bits = bits[:2], bits[2:]
        if len(first) == 2:
            low, high = first
            near, far, both = (swap(values, axis, mask) for mask in (low, high, low ^ high))
            values = (values + near) + (far + both)
        else:
            values = values + swap(values, axis, first[0])
    return values


def after(values, *earlier):
    return lax.optimization_barrier((values, *earlier))[0]


def join(chunks):
    return jnp.concatenate(chunks, axis=0)


def attend_forward(queries, keys, values, segment, places, width):
    length, heads_here, head_size = queries.shape
    contexts, logsums = [], []
    for first in range(0, length, width):
        part = slice(first, first + width)
        allowed = (segment[part, None] == segment[None, :]) & (places[part, None] >= places[None, :])
        scores = jnp.einsum(
            "qhe,khe->hqk", queries[part], keys, preferred_element_type=jnp.float32
        )
        scores = jnp.where(allowed[None], scores, -1e30)
        largest = jnp.max(scores, axis=-1, keepdims=True)
        exponent = jnp.exp(scores - largest)
        total = jnp.sum(exponent, axis=-1, keepdims=True)
        weights = (exponent / total).astype(jnp.bfloat16)
        context = jnp.einsum("hqk,khe->qhe", weights, values, preferred_element_type=jnp.float32)
        contexts.append(context.astype(jnp.bfloat16).reshape(width, heads_here * head_size))
        logsums.append(largest + jnp.log(total))
    return join(contexts), logsums


def attend_backward(queries, keys, values, grad_context, logsums, segment, places, width):
    length, heads_here, head_size = queries.shape
    grad_keys = jnp.zeros(keys.shape, jnp.float32)
    grad_values = jnp.zeros(keys.shape, jnp.float32)
    grad_queries = []
    for index, first in enumerate(range(0, length, width)):
        part = slice(first, first + width)
        allowed = (segment[part, None] == segment[None, :]) & (places[part, None] >= places[None, :])
        query_block, grad_block = queries[part], grad_context[part]
        scores = jnp.einsum("qhe,khe->hqk", query_block, keys, preferred_element_type=jnp.float32)
        scores = jnp.where(allowed[None], scores, -1e30)
        softmax_weights = jnp.exp(scores - logsums[index])
        grad_values = grad_values + jnp.einsum(
            "hqk,qhe->khe",
            softmax_weights.astype(jnp.bfloat16),
            grad_block,
            preferred_element_type=jnp.float32,
        )
        grad_weights = jnp.einsum(
            "qhe,khe->hqk", grad_block, values, preferred_element_type=jnp.float32
        )
        inner = jnp.sum(softmax_weights * grad_weights, axis=-1, keepdims=True)
        grad_scores = (softmax_weights * (grad_weights - inner)).astype(jnp.bfloat16)
        grad_query = jnp.einsum(
            "hqk,khe->qhe", grad_scores, keys, preferred_element_type=jnp.float32
        )
        grad_keys = grad_keys + jnp.einsum(
            "hqk,qhe->khe", grad_scores, query_block, preferred_element_type=jnp.float32
        )
        grad_queries.append(grad_query.astype(jnp.bfloat16).reshape(width, heads_here * head_size))
    return (
        join(grad_queries),
        grad_keys.astype(jnp.bfloat16).reshape(length, heads_here * head_size),
        grad_values.astype(jnp.bfloat16).reshape(length, heads_here * head_size),
    )


ROWS_DIM = (((0,), (0,)), ((), ()))
COLS_DIM = (((1,), (1,)), ((), ()))
f32 = jnp.float32


def dot(left, right):
    return jnp.dot(left, right, preferred_element_type=f32)


def dot_cols(left, right):
    return lax.dot_general(left, right, COLS_DIM, preferred_element_type=f32)


def dot_rows(left, right):
    return lax.dot_general(left, right, ROWS_DIM, preferred_element_type=f32)


def local(
    inputs,
    cotangent,
    doc_lengths,
    first_gain,
    first_shift,
    qkv_weight,
    qv_bias,
    out_weight,
    out_bias,
    second_gain,
    second_shift,
    up_weight,
    up_bias,
    down_weight,
    down_bias,
):
    rows_here = inputs.shape[0]
    group = lax.axis_size("mp")
    length = rows_here * group
    width = min(512, length)
    cols_here = qkv_weight.shape[2]
    heads_here = cols_here // HEAD_DIM
    factor = HEAD_DIM ** (-0.5)
    me = lax.axis_index("mp")
    order_a, order_b = orders("dp")
    ends = jnp.cumsum(doc_lengths[0])
    steps = jnp.arange(rows_here, dtype=jnp.int32)
    places = join([(me ^ r) * rows_here + steps for r in range(group)])
    segment = jnp.sum((places[:, None] >= ends[None, :]).astype(jnp.int32), axis=1)
    valid = (places[:rows_here] < ends[-1]).astype(f32)

    start_values = inputs.astype(f32)
    normed_one = layer_norm(start_values, first_gain, first_shift).astype(jnp.bfloat16)
    chunks_one = gather_chunks(normed_one)
    whole_qkv = gather_blocks(
        qkv_weight.reshape(qkv_weight.shape[0], 3 * cols_here), "dp", order_a
    )
    late_out = after(out_weight.T, whole_qkv)
    whole_out = gather_blocks(late_out, "dp", order_b)

    bias_chunks = jnp.concatenate(gather_chunks(up_bias))
    up_chunks = gather_chunks(after(up_weight, *chunks_one[1:]))
    down_chunks = gather_chunks(after(down_weight.T, *up_chunks[1:]))
    hidden_units = up_weight.shape[1] * group
    half = hidden_units // 2

    def halves(values):
        return values[..., :half], values[..., half:]

    whole_up = [
        gather_blocks(part, "dp", order)
        for part, order in zip(halves(jnp.concatenate(up_chunks, axis=1)), (order_a, order_b))
    ]
    late_down = after(jnp.concatenate(down_chunks, axis=1), *whole_up)
    whole_down = [
        gather_blocks(part, "dp", order)
        for part, order in zip(halves(late_down), (order_a, order_b))
    ]

    mixed = [dot(chunk, whole_qkv) for chunk in chunks_one]
    queries = join(
        [((m[:, :cols_here] + qv_bias[0]) * factor).astype(jnp.bfloat16) for m in mixed]
    ).reshape(length, heads_here, HEAD_DIM)
    keys_all = join([m[:, cols_here : 2 * cols_here].astype(jnp.bfloat16) for m in mixed]).reshape(
        length, heads_here, HEAD_DIM
    )
    values_all = join(
        [(m[:, 2 * cols_here :] + qv_bias[1]).astype(jnp.bfloat16) for m in mixed]
    ).reshape(length, heads_here, HEAD_DIM)
    context, logsum = attend_forward(queries, keys_all, values_all, segment, places, width)

    grad_out = cotangent.astype(f32) * valid[:, None]
    grad_out_low = grad_out.astype(jnp.bfloat16)

    def rows_of(values, r):
        return values[r * rows_here : (r + 1) * rows_here]

    hidden = (
        start_values
        + scatter_chunks(lambda r: dot_cols(rows_of(context, r), whole_out))
        + out_bias
    )
    normed_two = layer_norm(hidden, second_gain, second_shift).astype(jnp.bfloat16)
    active, grad_upper = [], []
    for up_part, down_part, bias in zip(whole_up, whole_down, halves(bias_chunks)):
        upper = dot(normed_two, up_part) + bias
        gate_value, gate_pull = jax.vjp(smooth_gate, upper)
        active.append(gate_value.astype(jnp.bfloat16))
        grad_active = dot(grad_out_low, down_part)
        grad_upper.append(gate_pull(grad_active)[0].astype(jnp.bfloat16))
    grad_normed_two = dot_cols(grad_upper[0], whole_up[0]) + dot_cols(grad_upper[1], whole_up[1])
    fed = dot_cols(active[0], whole_down[0]) + dot_cols(active[1], whole_down[1])
    result = (hidden + fed + down_bias).astype(jnp.bfloat16)

    norm_value, second_pull = jax.vjp(layer_norm, hidden, second_gain, second_shift)
    grad_hidden_norm, grad_second_gain, grad_second_shift = second_pull(grad_normed_two)
    grad_hidden = grad_out + grad_hidden_norm
    chunks_hidden = gather_chunks(grad_hidden.astype(jnp.bfloat16))
    grad_context = join([dot(chunk, whole_out).astype(jnp.bfloat16) for chunk in chunks_hidden])

    def own_shard(left, right_halves):
        parts = [
            scatter_product(left, right, "dp", order)
            for right, order in zip(right_halves, (order_a, order_b))
        ]
        whole = jnp.concatenate(parts, axis=1)
        size = hidden_units // group
        return scatter_chunks(lambda r: whole[:, r * size : (r + 1) * size])

    shard_up = own_shard(normed_two, grad_upper)
    shard_down = own_shard(grad_out_low, active).T
    shard_out = scatter_product(join(chunks_hidden), context, "dp", order_b).T
    bias_sums = jnp.concatenate([jnp.sum(part, axis=0, dtype=f32) for part in grad_upper])
    bias_sums = bias_sums.reshape(group, hidden_units // group)
    grad_up_bias = bias_sums[0]
    for r in range(1, group):
        grad_up_bias = grad_up_bias + swap(bias_sums[r], "mp", r)

    early = jnp.concatenate(
        [
            grad_second_gain,
            grad_second_shift,
            jnp.sum(grad_hidden, axis=0),
            jnp.sum(grad_out, axis=0),
        ]
    )
    model = first_gain.shape[0]
    early = sum_over(jnp.concatenate([sum_over(early, "mp"), grad_up_bias]), "dp")

    grad_queries, grad_keys, grad_values = attend_backward(
        queries,
        keys_all,
        values_all,
        grad_context.reshape(length, heads_here, HEAD_DIM),
        logsum,
        segment,
        places,
        width,
    )
    grad_queries = grad_queries * factor
    grad_mixed = jnp.concatenate([grad_queries, grad_keys, grad_values], axis=1)
    grad_normed_one = scatter_chunks(lambda r: dot_cols(rows_of(grad_mixed, r), whole_qkv))
    shard_qkv = scatter_product(join(chunks_one), grad_mixed, "dp", order_a)
    shard_qkv = shard_qkv.reshape(qkv_weight.shape)
    grad_qv_bias = jnp.concatenate(
        [jnp.sum(grad_queries, axis=0, dtype=f32), jnp.sum(grad_values, axis=0, dtype=f32)]
    )
    first_value, first_pull = jax.vjp(layer_norm, start_values, first_gain, first_shift)
    grad_start_norm, grad_first_gain, grad_first_shift = first_pull(grad_normed_one)
    grad_inputs = (grad_hidden + grad_start_norm).astype(jnp.bfloat16)
    late = sum_over(jnp.concatenate([grad_first_gain, grad_first_shift]), "mp")
    late = sum_over(jnp.concatenate([late, grad_qv_bias]), "dp")
    return (
        result,
        grad_inputs,
        late[:model],
        late[model : 2 * model],
        shard_qkv,
        late[2 * model :].reshape(2, cols_here),
        shard_out,
        early[2 * model : 3 * model],
        early[:model],
        early[model : 2 * model],
        shard_up,
        early[4 * model :],
        shard_down,
        early[3 * model : 4 * model],
    )


def solution(mesh):
    placed = (
        P(("dp", "mp"), None),
        P(("dp", "mp"), None),
        P("dp", None),
        P(),
        P(),
        P("dp", None, "mp"),
        P(None, "mp"),
        P("mp", "dp"),
        P(),
        P(),
        P(),
        P("dp", "mp"),
        P("mp"),
        P("mp", "dp"),
        P(),
    )
    return jax.shard_map(
        local,
        mesh=mesh,
        in_specs=placed,
        out_specs=(
            P(("dp", "mp"), None),
            P(("dp", "mp"), None),
            P(),
            P(),
            P("dp", None, "mp"),
            P(None, "mp"),
            P("mp", "dp"),
            P(),
            P(),
            P(),
            P("dp", "mp"),
            P("mp"),
            P("mp", "dp"),
            P(),
        ),
        check_vma=False,
    )
```

```python
import jax
import jax.numpy as jnp
from jax import lax
from jax.sharding import PartitionSpec as P

HEAD_DIM = 64


EPSILON = 1e-05


def layer_norm(values, gain, shift):
    center = values - jnp.mean(values, axis=-1, keepdims=True)
    spread = jnp.mean(center * center, axis=-1, keepdims=True)
    return center * lax.rsqrt(spread + EPSILON) * gain + shift


def smooth_gate(values):
    return jax.nn.gelu(values, approximate=True)


def swap(values, axis, mask):
    count = lax.axis_size(axis)
    return lax.ppermute(values, axis, [(i, i ^ mask) for i in range(count)])


def bits_of(axis):
    return [1 << k for k in range(lax.axis_size(axis).bit_length() - 1)]


def orders(axis):
    bits = bits_of(axis)
    return bits[1:] + bits[:1], bits[:0:-1] + bits[:1]


def gather_blocks(block, axis, order):
    me = lax.axis_index(axis)
    held = block[None]
    for bit in order:
        held = jnp.concatenate([held, swap(held, axis, bit)], axis=0)
    parts = []
    for j in range(lax.axis_size(axis)):
        relative = me ^ j
        slot = sum(((relative // bit) % 2) * (1 << k) for k, bit in enumerate(order))
        parts.append(lax.dynamic_index_in_dim(held, slot, 0, keepdims=False))
    return jnp.concatenate(parts, axis=0)


def first_half(left, right, axis, order):
    me = lax.axis_index(axis)
    bits = bits_of(axis)[::-1]
    rows = left.shape[1] // lax.axis_size(axis)
    split = left.reshape(left.shape[:1] + (2,) * len(bits) + (rows,))
    side = (me // order[-1]) % 2
    sent, kept = (
        dot_rows(
            lax.dynamic_index_in_dim(
                split, half, 1 + bits.index(order[-1]), keepdims=False
            ).reshape(left.shape[0], left.shape[1] // 2),
            right,
        )
        for half in (1 - side, side)
    )
    return sent.astype(jnp.bfloat16), kept


def halve(total, axis, order, step):
    me = lax.axis_index(axis)
    done = order[::-1][:step]
    bits = [bit for bit in bits_of(axis)[::-1] if bit not in done]
    bit = order[::-1][step]
    rows = total.shape[0] // (1 << len(bits))
    total = total.reshape((2,) * len(bits) + (rows,) + total.shape[1:])
    place, side = bits.index(bit), (me // bit) % 2
    sent, kept = (
        lax.dynamic_index_in_dim(total, half, place, keepdims=False).reshape(
            (rows << (len(bits) - 1),) + total.shape[len(bits) + 1 :]
        )
        for half in (1 - side, side)
    )
    return sent.astype(jnp.bfloat16), kept


def meet(halves, axis, order, step):
    sent, kept = halves
    return kept + swap(sent, axis, order[::-1][step]).astype(f32)


def scatter_product(left, right, axis, order):
    total = meet(first_half(left, right, axis, order), axis, order, 0)
    for step in range(1, len(order)):
        total = meet(halve(total, axis, order, step), axis, order, step)
    return total


def gather_chunks(chunk):
    return [chunk] + [swap(chunk, "mp", r) for r in range(1, lax.axis_size("mp"))]


def scatter_chunks(product):
    count = lax.axis_size("mp")
    arrived = [swap(product(r).astype(jnp.bfloat16), "mp", r) for r in range(count - 1, 0, -1)]
    total = product(0)
    for piece in arrived:
        total = total + piece.astype(jnp.float32)
    return total


def sum_over(values, axis):
    bits = bits_of(axis)
    while bits:
        first, bits = bits[:2], bits[2:]
        if len(first) == 2:
            low, high = first
            near, far, both = (swap(values, axis, mask) for mask in (low, high, low ^ high))
            values = (values + near) + (far + both)
        else:
            values = values + swap(values, axis, first[0])
    return values


def after(values, *earlier):
    return lax.optimization_barrier((values, *earlier))[0]


def join(chunks):
    return jnp.concatenate(chunks, axis=0)


def attend_forward(queries, keys, values, segment, places, width, between):
    length, heads_here, head_size = queries.shape
    contexts, logsums = [], []
    for first in range(0, length, width):
        part = slice(first, first + width)
        allowed = (segment[part, None] == segment[None, :]) & (places[part, None] >= places[None, :])
        scores = jnp.einsum(
            "qhe,khe->hqk", queries[part], keys, preferred_element_type=jnp.float32
        )
        scores = jnp.where(allowed[None], scores, -1e30)
        largest = jnp.max(scores, axis=-1, keepdims=True)
        exponent = jnp.exp(scores - largest)
        total = jnp.sum(exponent, axis=-1, keepdims=True)
        weights = (exponent / total).astype(jnp.bfloat16)
        context = jnp.einsum("hqk,khe->qhe", weights, values, preferred_element_type=jnp.float32)
        contexts.append(context.astype(jnp.bfloat16).reshape(width, heads_here * head_size))
        logsums.append(largest + jnp.log(total))
        if first == 0:
            between(contexts[0])
    return join(contexts), logsums


def attend_backward(
    queries, keys, values, grad_context, logsums, segment, places, width, between
):
    length, heads_here, head_size = queries.shape
    grad_keys = jnp.zeros(keys.shape, jnp.float32)
    grad_values = jnp.zeros(keys.shape, jnp.float32)
    grad_queries = []
    for index, first in enumerate(range(0, length, width)):
        part = slice(first, first + width)
        allowed = (segment[part, None] == segment[None, :]) & (places[part, None] >= places[None, :])
        query_block, grad_block = queries[part], grad_context[part]
        scores = jnp.einsum("qhe,khe->hqk", query_block, keys, preferred_element_type=jnp.float32)
        scores = jnp.where(allowed[None], scores, -1e30)
        softmax_weights = jnp.exp(scores - logsums[index])
        grad_values = grad_values + jnp.einsum(
            "hqk,qhe->khe",
            softmax_weights.astype(jnp.bfloat16),
            grad_block,
            preferred_element_type=jnp.float32,
        )
        grad_weights = jnp.einsum(
            "qhe,khe->hqk", grad_block, values, preferred_element_type=jnp.float32
        )
        inner = jnp.sum(softmax_weights * grad_weights, axis=-1, keepdims=True)
        grad_scores = (softmax_weights * (grad_weights - inner)).astype(jnp.bfloat16)
        grad_query = jnp.einsum(
            "hqk,khe->qhe", grad_scores, keys, preferred_element_type=jnp.float32
        )
        grad_keys = grad_keys + jnp.einsum(
            "hqk,qhe->khe", grad_scores, query_block, preferred_element_type=jnp.float32
        )
        grad_queries.append(grad_query.astype(jnp.bfloat16).reshape(width, heads_here * head_size))
        if first == 0:
            between(grad_queries[0])
    return (
        join(grad_queries),
        grad_keys.astype(jnp.bfloat16).reshape(length, heads_here * head_size),
        grad_values.astype(jnp.bfloat16).reshape(length, heads_here * head_size),
    )


ROWS_DIM = (((0,), (0,)), ((), ()))
COLS_DIM = (((1,), (1,)), ((), ()))
f32 = jnp.float32


def dot(left, right):
    return jnp.dot(left, right, preferred_element_type=f32)


def dot_cols(left, right):
    return lax.dot_general(left, right, COLS_DIM, preferred_element_type=f32)


def dot_rows(left, right):
    return lax.dot_general(left, right, ROWS_DIM, preferred_element_type=f32)


def local(
    inputs,
    cotangent,
    doc_lengths,
    first_gain,
    first_shift,
    qkv_weight,
    qv_bias,
    out_weight,
    out_bias,
    second_gain,
    second_shift,
    up_weight,
    up_bias,
    down_weight,
    down_bias,
):
    rows_here = inputs.shape[0]
    group = lax.axis_size("mp")
    length = rows_here * group
    width = min(512, length)
    cols_here = qkv_weight.shape[2]
    heads_here = cols_here // HEAD_DIM
    factor = HEAD_DIM ** (-0.5)
    me = lax.axis_index("mp")
    order_a, order_b = orders("dp")
    ends = jnp.cumsum(doc_lengths[0])
    steps = jnp.arange(rows_here, dtype=jnp.int32)
    places = join([(me ^ r) * rows_here + steps for r in range(group)])
    segment = jnp.sum((places[:, None] >= ends[None, :]).astype(jnp.int32), axis=1)
    valid = (places[:rows_here] < ends[-1]).astype(f32)

    start_values = inputs.astype(f32)
    normed_one = layer_norm(start_values, first_gain, first_shift).astype(jnp.bfloat16)
    chunks_one = gather_chunks(normed_one)
    shard = qkv_weight.reshape(qkv_weight.shape[0], 3 * cols_here)
    whole = gather_blocks(jnp.concatenate([shard, out_weight.T], axis=1), "dp", order_a)
    whole_qkv, whole_out = whole[:, : 3 * cols_here], whole[:, 3 * cols_here :]

    mixed = [dot(chunk, whole_qkv) for chunk in chunks_one]
    queries = join(
        [((m[:, :cols_here] + qv_bias[0]) * factor).astype(jnp.bfloat16) for m in mixed]
    ).reshape(length, heads_here, HEAD_DIM)
    keys_all = join([m[:, cols_here : 2 * cols_here].astype(jnp.bfloat16) for m in mixed]).reshape(
        length, heads_here, HEAD_DIM
    )
    values_all = join(
        [(m[:, 2 * cols_here :] + qv_bias[1]).astype(jnp.bfloat16) for m in mixed]
    ).reshape(length, heads_here, HEAD_DIM)

    hidden_units = up_weight.shape[1] * group
    half = hidden_units // 2

    def halves(values):
        return values[..., :half], values[..., half:]

    late_up, late_bias, late_down, queries, keys_all, values_all = lax.optimization_barrier(
        (up_weight, up_bias, down_weight.T, queries, keys_all, values_all)
    )
    up_chunks = gather_chunks(late_up)
    bias_parts = gather_chunks(late_bias)
    stages = {}

    def midway(block):
        *up, arrived = lax.optimization_barrier((*up_chunks, block))
        stages["up"] = [
            gather_blocks(part, "dp", order)
            for part, order in zip(halves(jnp.concatenate(up, axis=1)), (order_a, order_b))
        ]
        stages["down"] = gather_chunks(after(late_down, *up[1:], block))

    context, logsum = attend_forward(
        queries, keys_all, values_all, segment, places, width, midway
    )
    bias_chunks = jnp.concatenate(list(lax.optimization_barrier((*bias_parts, context)))[:-1])
    whole_up = stages["up"]
    down_chunks = lax.optimization_barrier((*stages["down"], context))[:-1]
    whole_down = [
        gather_blocks(part, "dp", order)
        for part, order in zip(halves(jnp.concatenate(down_chunks, axis=1)), (order_a, order_b))
    ]

    grad_out = cotangent.astype(f32) * valid[:, None]
    grad_out_low = grad_out.astype(jnp.bfloat16)

    def rows_of(values, r):
        return values[r * rows_here : (r + 1) * rows_here]

    hidden = (
        start_values
        + scatter_chunks(lambda r: dot_cols(rows_of(context, r), whole_out))
        + out_bias
    )
    normed_two = layer_norm(hidden, second_gain, second_shift).astype(jnp.bfloat16)
    active, grad_upper = [], []
    for up_part, down_part, bias in zip(whole_up, whole_down, halves(bias_chunks)):
        upper = dot(normed_two, up_part) + bias
        gate_value, gate_pull = jax.vjp(smooth_gate, upper)
        active.append(gate_value.astype(jnp.bfloat16))
        grad_active = dot(grad_out_low, down_part)
        grad_upper.append(gate_pull(grad_active)[0].astype(jnp.bfloat16))
    grad_normed_two = dot_cols(grad_upper[0], whole_up[0]) + dot_cols(grad_upper[1], whole_up[1])
    fed = dot_cols(active[0], whole_down[0]) + dot_cols(active[1], whole_down[1])
    result = (hidden + fed + down_bias).astype(jnp.bfloat16)

    norm_value, second_pull = jax.vjp(layer_norm, hidden, second_gain, second_shift)
    grad_hidden_norm, grad_second_gain, grad_second_shift = second_pull(grad_normed_two)
    grad_hidden = grad_out + grad_hidden_norm
    chunks_hidden = gather_chunks(grad_hidden.astype(jnp.bfloat16))
    grad_context = join([dot(chunk, whole_out).astype(jnp.bfloat16) for chunk in chunks_hidden])

    both = (order_a, order_b) * 2
    firsts = [
        first_half(left, right, "dp", order)
        for (left, right), order in zip(
            [(normed_two, right) for right in grad_upper]
            + [(grad_out_low, right) for right in active],
            both,
        )
    ]
    firsts, grad_context = lax.optimization_barrier((firsts, grad_context))
    sums = [meet(pair, "dp", order, 0) for pair, order in zip(firsts, both)]
    out_sum = scatter_product(join(chunks_hidden), context, "dp", order_b)

    def step_sums(step, value):
        sums[:] = lax.optimization_barrier((sums, value))[0]
        if step < len(order_a):
            sums[:] = [
                meet(halve(total, "dp", order, step), "dp", order, step)
                for total, order in zip(sums, both)
            ]

    bias_sums = jnp.concatenate([jnp.sum(part, axis=0, dtype=f32) for part in grad_upper])
    bias_sums = bias_sums.reshape(group, hidden_units // group)
    grad_up_bias = bias_sums[0]
    for r in range(1, group):
        grad_up_bias = grad_up_bias + swap(bias_sums[r], "mp", r)

    early = jnp.concatenate(
        [
            grad_second_gain,
            grad_second_shift,
            jnp.sum(grad_hidden, axis=0),
            jnp.sum(grad_out, axis=0),
        ]
    )
    model = first_gain.shape[0]
    early = sum_over(jnp.concatenate([sum_over(early, "mp"), grad_up_bias]), "dp")

    grad_queries, grad_keys, grad_values = attend_backward(
        queries,
        keys_all,
        values_all,
        grad_context.reshape(length, heads_here, HEAD_DIM),
        logsum,
        segment,
        places,
        width,
        lambda block: step_sums(1, block),
    )
    grad_queries = grad_queries * factor
    grad_mixed = jnp.concatenate([grad_queries, grad_keys, grad_values], axis=1)
    for step in range(2, len(order_a)):
        step_sums(step, grad_mixed)
    grad_normed_one = scatter_chunks(lambda r: dot_cols(rows_of(grad_mixed, r), whole_qkv))
    step_sums(len(order_a), grad_normed_one)
    size = hidden_units // group

    def own_shard(parts):
        both_halves = jnp.concatenate(parts, axis=1)
        return scatter_chunks(lambda r: both_halves[:, r * size : (r + 1) * size])

    shard_up, shard_down, shard_out = own_shard(sums[:2]), own_shard(sums[2:]).T, out_sum.T
    shard_qkv = scatter_product(join(chunks_one), grad_mixed, "dp", order_a)
    shard_qkv = shard_qkv.reshape(qkv_weight.shape)
    grad_qv_bias = jnp.concatenate(
        [jnp.sum(grad_queries, axis=0, dtype=f32), jnp.sum(grad_values, axis=0, dtype=f32)]
    )
    first_value, first_pull = jax.vjp(layer_norm, start_values, first_gain, first_shift)
    grad_start_norm, grad_first_gain, grad_first_shift = first_pull(grad_normed_one)
    grad_inputs = (grad_hidden + grad_start_norm).astype(jnp.bfloat16)
    late = sum_over(jnp.concatenate([grad_first_gain, grad_first_shift]), "mp")
    late = sum_over(jnp.concatenate([late, grad_qv_bias]), "dp")
    return (
        result,
        grad_inputs,
        late[:model],
        late[model : 2 * model],
        shard_qkv,
        late[2 * model :].reshape(2, cols_here),
        shard_out,
        early[2 * model : 3 * model],
        early[:model],
        early[model : 2 * model],
        shard_up,
        early[4 * model :],
        shard_down,
        early[3 * model : 4 * model],
    )


def solution(mesh):
    placed = (
        P(("dp", "mp"), None),
        P(("dp", "mp"), None),
        P("dp", None),
        P(),
        P(),
        P("dp", None, "mp"),
        P(None, "mp"),
        P("mp", "dp"),
        P(),
        P(),
        P(),
        P("dp", "mp"),
        P("mp"),
        P("mp", "dp"),
        P(),
    )
    return jax.shard_map(
        local,
        mesh=mesh,
        in_specs=placed,
        out_specs=(
            P(("dp", "mp"), None),
            P(("dp", "mp"), None),
            P(),
            P(),
            P("dp", None, "mp"),
            P(None, "mp"),
            P("mp", "dp"),
            P(),
            P(),
            P(),
            P("dp", "mp"),
            P("mp"),
            P("mp", "dp"),
            P(),
        ),
        check_vma=False,
    )
```

```python
import jax
import jax.numpy as jnp
from jax import lax
from jax.sharding import PartitionSpec as P

HEAD_DIM = 64


EPSILON = 1e-05


def layer_norm(values, gain, shift):
    center = values - jnp.mean(values, axis=-1, keepdims=True)
    spread = jnp.mean(center * center, axis=-1, keepdims=True)
    return center * lax.rsqrt(spread + EPSILON) * gain + shift


def smooth_gate(values):
    return jax.nn.gelu(values, approximate=True)


def swap(values, axis, mask):
    count = lax.axis_size(axis)
    return lax.ppermute(values, axis, [(i, i ^ mask) for i in range(count)])


def bits_of(axis):
    return [1 << k for k in range(lax.axis_size(axis).bit_length() - 1)]


def orders(axis):
    bits = bits_of(axis)
    return bits[1:] + bits[:1], bits[:0:-1] + bits[:1]


def gather_blocks(block, axis, order):
    me = lax.axis_index(axis)
    held = block[None]
    for bit in order:
        held = jnp.concatenate([held, swap(held, axis, bit)], axis=0)
    parts = []
    for j in range(lax.axis_size(axis)):
        relative = me ^ j
        slot = sum(((relative // bit) % 2) * (1 << k) for k, bit in enumerate(order))
        parts.append(lax.dynamic_index_in_dim(held, slot, 0, keepdims=False))
    return jnp.concatenate(parts, axis=0)


def first_half(left, right, axis, order):
    me = lax.axis_index(axis)
    bits = bits_of(axis)[::-1]
    rows = left.shape[1] // lax.axis_size(axis)
    split = left.reshape(left.shape[:1] + (2,) * len(bits) + (rows,))
    side = (me // order[-1]) % 2
    sent, kept = (
        dot_rows(
            lax.dynamic_index_in_dim(
                split, half, 1 + bits.index(order[-1]), keepdims=False
            ).reshape(left.shape[0], left.shape[1] // 2),
            right,
        )
        for half in (1 - side, side)
    )
    return sent.astype(jnp.bfloat16), kept


def halve(total, axis, order, step):
    me = lax.axis_index(axis)
    done = order[::-1][:step]
    bits = [bit for bit in bits_of(axis)[::-1] if bit not in done]
    bit = order[::-1][step]
    rows = total.shape[0] // (1 << len(bits))
    total = total.reshape((2,) * len(bits) + (rows,) + total.shape[1:])
    place, side = bits.index(bit), (me // bit) % 2
    sent, kept = (
        lax.dynamic_index_in_dim(total, half, place, keepdims=False).reshape(
            (rows << (len(bits) - 1),) + total.shape[len(bits) + 1 :]
        )
        for half in (1 - side, side)
    )
    return sent.astype(jnp.bfloat16), kept


def meet(halves, axis, order, step):
    sent, kept = halves
    return kept + swap(sent, axis, order[::-1][step]).astype(f32)


def scatter_product(left, right, axis, order):
    total = meet(first_half(left, right, axis, order), axis, order, 0)
    for step in range(1, len(order)):
        total = meet(halve(total, axis, order, step), axis, order, step)
    return total


def gather_chunks(chunk):
    return [chunk] + [swap(chunk, "mp", r) for r in range(1, lax.axis_size("mp"))]


def scatter_chunks(product):
    count = lax.axis_size("mp")
    arrived = [swap(product(r).astype(jnp.bfloat16), "mp", r) for r in range(count - 1, 0, -1)]
    total = product(0)
    for piece in arrived:
        total = total + piece.astype(jnp.float32)
    return total


def sum_over(values, axis):
    bits = bits_of(axis)
    while bits:
        first, bits = bits[:2], bits[2:]
        if len(first) == 2:
            low, high = first
            near, far, both = (swap(values, axis, mask) for mask in (low, high, low ^ high))
            values = (values + near) + (far + both)
        else:
            values = values + swap(values, axis, first[0])
    return values


def tie(values, *earlier):
    zero = sum(jnp.minimum(jnp.abs(e[(0,) * e.ndim].astype(f32)), 0.0) for e in earlier)
    return (values.astype(f32) + zero).astype(values.dtype)


def join(chunks):
    return jnp.concatenate(chunks, axis=0)


def attend_forward(queries, keys, values, segment, places, width):
    length, heads_here, head_size = queries.shape
    contexts, logsums = [], []
    for first in range(0, length, width):
        part = slice(first, first + width)
        allowed = (segment[part, None] == segment[None, :]) & (places[part, None] >= places[None, :])
        scores = jnp.einsum(
            "qhe,khe->hqk", queries[part], keys, preferred_element_type=jnp.float32
        )
        scores = jnp.where(allowed[None], scores, -1e30)
        largest = jnp.max(scores, axis=-1, keepdims=True)
        exponent = jnp.exp(scores - largest)
        total = jnp.sum(exponent, axis=-1, keepdims=True)
        weights = (exponent / total).astype(jnp.bfloat16)
        context = jnp.einsum("hqk,khe->qhe", weights, values, preferred_element_type=jnp.float32)
        contexts.append(context.astype(jnp.bfloat16).reshape(width, heads_here * head_size))
        logsums.append(largest + jnp.log(total))
    return join(contexts), logsums


def attend_backward(
    queries, keys, values, grad_context, logsums, segment, places, width
):
    length, heads_here, head_size = queries.shape
    grad_keys = jnp.zeros(keys.shape, jnp.float32)
    grad_values = jnp.zeros(keys.shape, jnp.float32)
    grad_queries = []
    for index, first in enumerate(range(0, length, width)):
        part = slice(first, first + width)
        allowed = (segment[part, None] == segment[None, :]) & (places[part, None] >= places[None, :])
        query_block, grad_block = queries[part], grad_context[part]
        scores = jnp.einsum("qhe,khe->hqk", query_block, keys, preferred_element_type=jnp.float32)
        scores = jnp.where(allowed[None], scores, -1e30)
        softmax_weights = jnp.exp(scores - logsums[index])
        grad_values = grad_values + jnp.einsum(
            "hqk,qhe->khe",
            softmax_weights.astype(jnp.bfloat16),
            grad_block,
            preferred_element_type=jnp.float32,
        )
        grad_weights = jnp.einsum(
            "qhe,khe->hqk", grad_block, values, preferred_element_type=jnp.float32
        )
        inner = jnp.sum(softmax_weights * grad_weights, axis=-1, keepdims=True)
        grad_scores = (softmax_weights * (grad_weights - inner)).astype(jnp.bfloat16)
        grad_query = jnp.einsum(
            "hqk,khe->qhe", grad_scores, keys, preferred_element_type=jnp.float32
        )
        grad_keys = grad_keys + jnp.einsum(
            "hqk,qhe->khe", grad_scores, query_block, preferred_element_type=jnp.float32
        )
        grad_queries.append(grad_query.astype(jnp.bfloat16).reshape(width, heads_here * head_size))
    return (
        join(grad_queries),
        grad_keys.astype(jnp.bfloat16).reshape(length, heads_here * head_size),
        grad_values.astype(jnp.bfloat16).reshape(length, heads_here * head_size),
    )


ROWS_DIM = (((0,), (0,)), ((), ()))
COLS_DIM = (((1,), (1,)), ((), ()))
f32 = jnp.float32


def dot(left, right):
    return jnp.dot(left, right, preferred_element_type=f32)


def dot_cols(left, right):
    return lax.dot_general(left, right, COLS_DIM, preferred_element_type=f32)


def dot_rows(left, right):
    return lax.dot_general(left, right, ROWS_DIM, preferred_element_type=f32)


def local(
    inputs,
    cotangent,
    doc_lengths,
    first_gain,
    first_shift,
    qkv_weight,
    qv_bias,
    out_weight,
    out_bias,
    second_gain,
    second_shift,
    up_weight,
    up_bias,
    down_weight,
    down_bias,
):
    rows_here = inputs.shape[0]
    group = lax.axis_size("mp")
    length = rows_here * group
    width = min(512, length)
    cols_here = qkv_weight.shape[2]
    heads_here = cols_here // HEAD_DIM
    factor = HEAD_DIM ** (-0.5)
    me = lax.axis_index("mp")
    order_a, order_b = orders("dp")
    ends = jnp.cumsum(doc_lengths[0])
    steps = jnp.arange(rows_here, dtype=jnp.int32)
    places = join([(me ^ r) * rows_here + steps for r in range(group)])
    segment = jnp.sum((places[:, None] >= ends[None, :]).astype(jnp.int32), axis=1)
    valid = (places[:rows_here] < ends[-1]).astype(f32)

    start_values = inputs.astype(f32)
    normed_one = layer_norm(start_values, first_gain, first_shift).astype(jnp.bfloat16)
    chunks_one = gather_chunks(normed_one)
    shard = qkv_weight.reshape(qkv_weight.shape[0], 3 * cols_here)
    whole = gather_blocks(jnp.concatenate([shard, out_weight.T], axis=1), "dp", order_a)
    whole_qkv, whole_out = whole[:, : 3 * cols_here], whole[:, 3 * cols_here :]

    mixed = [dot(chunk, whole_qkv) for chunk in chunks_one]
    queries = join(
        [((m[:, :cols_here] + qv_bias[0]) * factor).astype(jnp.bfloat16) for m in mixed]
    ).reshape(length, heads_here, HEAD_DIM)
    keys_all = join([m[:, cols_here : 2 * cols_here].astype(jnp.bfloat16) for m in mixed]).reshape(
        length, heads_here, HEAD_DIM
    )
    values_all = join(
        [(m[:, 2 * cols_here :] + qv_bias[1]).astype(jnp.bfloat16) for m in mixed]
    ).reshape(length, heads_here, HEAD_DIM)

    hidden_units = up_weight.shape[1] * group
    half = hidden_units // 2

    def halves(values):
        return values[..., :half], values[..., half:]

    up_chunks = gather_chunks(tie(up_weight, mixed[-1]))
    down_chunks = gather_chunks(tie(down_weight.T, mixed[-1]))
    bias_chunks = jnp.concatenate(gather_chunks(tie(up_bias, mixed[-1])))
    whole_up, whole_down = (
        [
            gather_blocks(part, "dp", order)
            for part, order in zip(halves(jnp.concatenate(chunks, axis=1)), (order_a, order_b))
        ]
        for chunks in (up_chunks, down_chunks)
    )
    context, logsum = attend_forward(queries, keys_all, values_all, segment, places, width)
    context = tie(context, *up_chunks[1:], *down_chunks[1:])

    grad_out = cotangent.astype(f32) * valid[:, None]
    grad_out_low = grad_out.astype(jnp.bfloat16)

    def rows_of(values, r):
        return values[r * rows_here : (r + 1) * rows_here]

    hidden = (
        start_values
        + scatter_chunks(lambda r: dot_cols(rows_of(context, r), whole_out))
        + out_bias
    )
    normed_two = layer_norm(hidden, second_gain, second_shift).astype(jnp.bfloat16)
    active, grad_upper = [], []
    for up_part, down_part, bias in zip(whole_up, whole_down, halves(bias_chunks)):
        upper = dot(normed_two, up_part) + bias
        gate_value, gate_pull = jax.vjp(smooth_gate, upper)
        active.append(gate_value.astype(jnp.bfloat16))
        grad_active = dot(grad_out_low, down_part)
        grad_upper.append(gate_pull(grad_active)[0].astype(jnp.bfloat16))
    grad_normed_two = dot_cols(grad_upper[0], whole_up[0]) + dot_cols(grad_upper[1], whole_up[1])
    fed = dot_cols(active[0], whole_down[0]) + dot_cols(active[1], whole_down[1])
    result = (hidden + fed + down_bias).astype(jnp.bfloat16)

    norm_value, second_pull = jax.vjp(layer_norm, hidden, second_gain, second_shift)
    grad_hidden_norm, grad_second_gain, grad_second_shift = second_pull(grad_normed_two)
    grad_hidden = grad_out + grad_hidden_norm
    chunks_hidden = gather_chunks(grad_hidden.astype(jnp.bfloat16))
    grad_context = join([dot(chunk, whole_out).astype(jnp.bfloat16) for chunk in chunks_hidden])

    both = (order_a, order_b) * 2
    firsts = [
        first_half(left, right, "dp", order)
        for (left, right), order in zip(
            [(normed_two, right) for right in grad_upper]
            + [(grad_out_low, right) for right in active],
            both,
        )
    ]
    sums = [meet(pair, "dp", order, 0) for pair, order in zip(firsts, both)]
    out_sum = scatter_product(join(chunks_hidden), context, "dp", order_b)

    grad_context = join([grad_context[:width], tie(grad_context[width:], *sums)])
    for step in range(1, len(order_a)):
        sums = [
            meet(halve(total, "dp", order, step), "dp", order, step)
            for total, order in zip(sums, both)
        ]

    bias_sums = jnp.concatenate([jnp.sum(part, axis=0, dtype=f32) for part in grad_upper])
    bias_sums = bias_sums.reshape(group, hidden_units // group)
    grad_up_bias = bias_sums[0]
    for r in range(1, group):
        grad_up_bias = grad_up_bias + swap(bias_sums[r], "mp", r)

    early = jnp.concatenate(
        [
            grad_second_gain,
            grad_second_shift,
            jnp.sum(grad_hidden, axis=0),
            jnp.sum(grad_out, axis=0),
        ]
    )
    model = first_gain.shape[0]
    early = sum_over(jnp.concatenate([sum_over(early, "mp"), grad_up_bias]), "dp")

    grad_queries, grad_keys, grad_values = attend_backward(
        queries,
        keys_all,
        values_all,
        grad_context.reshape(length, heads_here, HEAD_DIM),
        logsum,
        segment,
        places,
        width,
    )
    grad_queries = grad_queries * factor
    grad_mixed = jnp.concatenate([grad_queries, grad_keys, grad_values], axis=1)
    grad_normed_one = scatter_chunks(lambda r: dot_cols(rows_of(grad_mixed, r), whole_qkv))
    size = hidden_units // group

    def own_shard(parts):
        both_halves = jnp.concatenate(parts, axis=1)
        return scatter_chunks(lambda r: both_halves[:, r * size : (r + 1) * size])

    shard_up, shard_down, shard_out = own_shard(sums[:2]), own_shard(sums[2:]).T, out_sum.T
    shard_qkv = scatter_product(join(chunks_one), grad_mixed, "dp", order_a)
    shard_qkv = shard_qkv.reshape(qkv_weight.shape)
    grad_qv_bias = jnp.concatenate(
        [jnp.sum(grad_queries, axis=0, dtype=f32), jnp.sum(grad_values, axis=0, dtype=f32)]
    )
    first_value, first_pull = jax.vjp(layer_norm, start_values, first_gain, first_shift)
    grad_start_norm, grad_first_gain, grad_first_shift = first_pull(grad_normed_one)
    grad_inputs = (grad_hidden + grad_start_norm).astype(jnp.bfloat16)
    late = tie(jnp.concatenate([grad_first_gain, grad_first_shift]), *sums)
    late = sum_over(late, "mp")
    late = sum_over(jnp.concatenate([late, grad_qv_bias]), "dp")
    return (
        result,
        grad_inputs,
        late[:model],
        late[model : 2 * model],
        shard_qkv,
        late[2 * model :].reshape(2, cols_here),
        shard_out,
        early[2 * model : 3 * model],
        early[:model],
        early[model : 2 * model],
        shard_up,
        early[4 * model :],
        shard_down,
        early[3 * model : 4 * model],
    )


def solution(mesh):
    placed = (
        P(("dp", "mp"), None),
        P(("dp", "mp"), None),
        P("dp", None),
        P(),
        P(),
        P("dp", None, "mp"),
        P(None, "mp"),
        P("mp", "dp"),
        P(),
        P(),
        P(),
        P("dp", "mp"),
        P("mp"),
        P("mp", "dp"),
        P(),
    )
    return jax.shard_map(
        local,
        mesh=mesh,
        in_specs=placed,
        out_specs=(
            P(("dp", "mp"), None),
            P(("dp", "mp"), None),
            P(),
            P(),
            P("dp", None, "mp"),
            P(None, "mp"),
            P("mp", "dp"),
            P(),
            P(),
            P(),
            P("dp", "mp"),
            P("mp"),
            P("mp", "dp"),
            P(),
        ),
        check_vma=False,
    )
```
